256 devices in a mesh: rep: 16 (over y, z_lo), tp: 16 (over x, z_hi, core).
Axes of the slice: x: 4, y: 4, z: 8 (z_hi: 2, z_lo: 4; z = z_hi * 4 + z_lo), core: 2. Of those that a mesh axis runs over, the one named last changes fastest.
Arguments:
- replica_weights: bfloat16 [16, 7168, 3584], P('rep', 'tp'), may hold values from -6 to 6
- slow_weights: float32 [7168, 3584], P('tp', 'rep'), may hold values from -6 to 6
- momentum: float32 [7168, 3584], P('tp', 'rep'), may hold values from -2 to 2
- hidden: bfloat16 [16, 2, 256, 7168], P('rep', None, None, 'tp'), may hold values from -6 to 6
- residual: bfloat16 [16, 2, 3584, 256], P('rep', None, 'tp'), may hold values from -60 to 60
- target: bfloat16 [16, 2, 3584, 256], P('rep', None, 'tp'), may hold values from -6 to 6
- arrival: int32 [16], replicated, may hold values from 0 to 15, each once
- staleness: int32 [16], replicated, may hold values from 0 to 4, as said below
- live: int32 [16], replicated, may hold values from 1 to 256, 2048 in all
Outputs:
- returned: bfloat16 [16, 7168, 3584], P('rep', 'tp')
- slow_after: float32 [7168, 3584], P('tp', 'rep')
- momentum_after: float32 [7168, 3584], P('tp', 'rep')
The draws below stay inside these ranges and needn't reach their ends.
Inputs may be any that keep to these rules, and one draw needn't show every extreme that they name: `staleness`: every value from 0 to 4 occurs. `arrival`: a permutation of the replicas. The live counts sum to 2048, and some replica has all 256 tokens live.
All inputs are finite; a program needn't handle non-finite values.
Results may differ from the reference program's by a relative error of at most 0.008.
Values may be sent and summed in bfloat16 or wider, within the bound.
No kernel may reach another device: no remote copies, remote signals or barrier semaphores. Data moves between devices by JAX's collectives and lax.ppermute only.
A program may use at most 128 MiB of HBM per device.

```python
import math
import jax
import jax.numpy as jnp
import numpy as np
from jax import lax

D = 3584
FF = 7168
TOK = 256
ITERS = 2
N_REPLICAS = 16
BLOCK_FF = 448
N_TP = 16


def draw_residual(key, part):
    key = jax.random.fold_in(key, 11)
    key_base, key_rows = jax.random.split(key, 2)
    shape = (N_REPLICAS, ITERS, D, TOK)
    columns = 0.1 * jnp.power(10.0, jnp.arange(D, dtype=jnp.float32) / D)
    base = jnp.clip(jax.random.normal(key_base, shape, jnp.float32), -6.0, 6.0)
    rows = jnp.exp(jax.random.uniform(key_rows, (N_REPLICAS, ITERS, 1, TOK), jnp.float32, 0.0, math.log(10.0)))
    values = base * columns[None, None, :, None] * rows
    return jnp.clip(values, -60.0, 60.0).astype(jnp.bfloat16)


def draw_staleness(key, part):
    key = jax.random.fold_in(key, 23)
    order = jax.random.permutation(key, N_REPLICAS)
    return (order % 5).astype(jnp.int32)


def block_scale(rng, dims, cuts, low, high):
    factor_of, own = 1.0, jax.random.fold_in(rng, 6)
    for dim, shards_of in cuts:
        steps = jnp.exp(jax.random.uniform(jax.random.fold_in(own, dim), (shards_of,), jnp.float32, low / len(cuts), high / len(cuts)))
        factor_of = factor_of * jnp.repeat(steps, dims[dim] // shards_of).reshape([-1 if axis == dim else 1 for axis in range(len(dims))])
    return factor_of


def length_profile(amount, total, bound, lean):
    weights = [(1 << 20) // math.isqrt(grade ** lean) + 1 for grade in range(2, amount + 1)]
    rest, counts = total - bound - (amount - 1), [1] * (amount - 1)
    while rest > 0:
        movable = [i for i in range(amount - 1) if counts[i] < bound]
        whole, budget = sum([weights[i] for i in movable]), rest
        for i in movable:
            more = min(bound - counts[i], max(1, budget * weights[i] // whole), rest)
            counts[i] = counts[i] + more
            rest = rest - more
    return np.array([bound] + counts)


def ragged_sizes(own_key, amount, total, bound, slope):
    if amount == 2:
        one = jax.random.randint(own_key, (), max(1, total - bound), min(bound, total - 1) + 1)
        return jnp.stack([one, total - one])
    tallies = jnp.asarray(length_profile(amount, total, bound, slope), jnp.int32)
    twos = (amount - 1) // 2
    giver, taker = tallies[1:1 + 2 * twos:2], tallies[2:2 + 2 * twos:2]
    room = jnp.minimum(giver - 1, bound - taker)
    passed = jax.random.randint(jax.random.fold_in(own_key, 1), (twos,), 0, 1 << 20) % (room + 1)
    tallies = tallies.at[1:1 + 2 * twos:2].set(giver - passed).at[2:2 + 2 * twos:2].set(taker + passed)
    return tallies[jax.random.permutation(jax.random.fold_in(own_key, 2), amount)]


def scatter_about(rng, dims, spread, limit, cuts=(), kind=jnp.bfloat16):
    values = spread * jax.random.normal(rng, dims, jnp.float32)
    if cuts:
        values = values * block_scale(rng, dims, cuts, -0.22, 0.18)
    return jnp.clip(values, -limit, limit).astype(kind)


def setup_inputs(seed: int = 0) -> dict:
    streams_of = jax.random.split(jax.random.key(seed), 10)
    return {
        "replica_weights": scatter_about(streams_of[0], (N_REPLICAS, FF, D), 1.0, 6.0, ((0, 16), (1, 16))),
        "slow_weights": scatter_about(streams_of[1], (FF, D), 1.0, 6.0, ((0, 16), (1, 16)), jnp.float32),
        "momentum": scatter_about(streams_of[2], (FF, D), 0.3, 2.0, ((0, 16), (1, 16)), jnp.float32),
        "hidden": scatter_about(streams_of[3], (N_REPLICAS, ITERS, TOK, FF), 1.0, 6.0, ((0, 16), (3, 16))),
        "residual": draw_residual(jax.random.fold_in(streams_of[9], 71), 0),
        "target": scatter_about(streams_of[5], (N_REPLICAS, ITERS, D, TOK), 1.0, 6.0, ((0, 16), (2, 16))),
        "arrival": jax.random.permutation(streams_of[6], N_REPLICAS).astype(jnp.int32),
        "staleness": draw_staleness(jax.random.fold_in(streams_of[9], 71), 0),
        "live": ragged_sizes(streams_of[8], N_REPLICAS, N_REPLICAS * TOK // 2, TOK, 2).astype(jnp.int32),
    }


inner_rate = 2.0
outer_rate = 0.7
momentum_decay = 0.9
epsilon = 1e-06

def inner_delta(operands):
    weights, features_all, residual_all, target_all, live_count = operands
    inv_width = 1.0 / math.sqrt(FF)
    current = weights.astype(jnp.float32)
    token_mask = (jnp.arange(TOK, dtype=jnp.int32) < live_count).astype(jnp.float32)
    for inner_step in range(ITERS):
        features = features_all[inner_step]
        narrow = current.astype(jnp.bfloat16)
        blocks = jnp.einsum('tbf,bfd->bdt', features.reshape(TOK, N_TP, BLOCK_FF).astype(jnp.float32), narrow.reshape(N_TP, BLOCK_FF, D).astype(jnp.float32)) * inv_width
        output = lax.optimization_barrier(jnp.sum(blocks.astype(jnp.bfloat16).astype(jnp.float32), axis=0))
        summed = residual_all[inner_step].astype(jnp.float32) + output
        target_now = target_all[inner_step].astype(jnp.float32)
        rms = jnp.sqrt(lax.optimization_barrier(jnp.sum(summed * summed, axis=0)) / D + epsilon)
        along = lax.optimization_barrier(jnp.sum(target_now * summed, axis=0)) / D / rms
        grad_rows = (token_mask * (target_now - summed / rms * along) / rms).astype(jnp.bfloat16)
        update = jnp.dot(features.T, grad_rows.T, preferred_element_type=jnp.float32)
        current = current - inner_rate * inv_width * update
    return (weights.astype(jnp.float32) - current).astype(jnp.bfloat16)

def reference(replica_weights, slow_weights, momentum, hidden, residual, target, arrival, staleness, live):
    deltas = lax.map(inner_delta, (replica_weights, hidden, residual, target, live))
    factors = 1.0 / (1.0 + staleness.astype(jnp.float32))

    def advance(carry, inputs):
        slow_now, held = carry
        which, factor = inputs
        outer_grad = lax.dynamic_index_in_dim(deltas, which, 0, keepdims=False).astype(jnp.float32) * factor
        held = momentum_decay * held + outer_grad
        slow_now = slow_now - outer_rate * (outer_grad + momentum_decay * held)
        return ((slow_now, held), slow_now.astype(jnp.bfloat16))
    (slow_after, momentum_after), results = lax.scan(advance, (slow_weights, momentum), (arrival, factors))
    slots = jnp.arange(N_REPLICAS, dtype=jnp.int32)
    position = lax.optimization_barrier(jnp.sum(jnp.where(arrival[None, :] == slots[:, None], slots[None, :], 0), axis=1)).astype(jnp.int32)
    returned = jnp.take(results, position, axis=0)
    return (returned, slow_after, momentum_after)
```

```python
import itertools
import math

import jax
import jax.numpy as jnp
from jax import lax
from jax.experimental import pallas as pl
from jax.experimental.pallas import tpu as pltpu
from jax.sharding import Mesh
from jax.sharding import PartitionSpec as P

D = 3584
FF = 7168
TOK = 256
ITERS = 2
REPLICAS = 16
ROWS = 448
COLS = 224
WIDE = 896
PACKED = 784

inner_rate = 2.0
outer_rate = 0.7
momentum_decay = 0.9
epsilon = 1e-06

AXES = ("y", "b", "a", "x", "h", "c")
SIZES = (4, 2, 2, 4, 2, 2)
F32 = jnp.float32
BF16 = jnp.bfloat16


def flat(*where):
    index = 0
    for size, place in zip(SIZES, where):
        index = index * size + place
    return index


def devices():
    return itertools.product(*map(range, SIZES))


def swap(value, axis):
    return lax.ppermute(value, axis, [(0, 1), (1, 0)])


def ring(value, axis, mask):
    return lax.ppermute(value, axis, [(i, i ^ mask) for i in range(4)])


def line(value, mask):
    return lax.ppermute(value, ("b", "a"), [(i, i ^ mask) for i in range(4)])


def pick(array, index, axis=0):
    return lax.dynamic_index_in_dim(array, index, axis, keepdims=False)


def forward_kernel(rows_ref, weights_ref, out_ref):
    out_ref[0] = (
        jnp.dot(rows_ref[...], weights_ref[...], preferred_element_type=F32)
        * (1.0 / math.sqrt(FF))
    ).astype(BF16)


def forward(rows, weights):
    count = rows.shape[0]
    return pl.pallas_call(
        forward_kernel,
        grid=(4,),
        in_specs=[
            pl.BlockSpec((count, ROWS), lambda i: (0, 0)),
            pl.BlockSpec((ROWS, WIDE), lambda i: (0, i)),
        ],
        out_specs=pl.BlockSpec((1, count, WIDE), lambda i: (i, 0, 0)),
        out_shape=jax.ShapeDtypeStruct((4, count, WIDE), BF16),
        cost_estimate=pl.CostEstimate(
            flops=2 * count * ROWS * D, bytes_accessed=2 * ROWS * D, transcendentals=0
        ),
        compiler_params=pltpu.CompilerParams(vmem_limit_bytes=32 << 20),
        name="forward",
    )(rows, weights)


def reduce_tokens(keep, send, extra_keep, extra_send, x, h):
    got = swap(send, "c")
    extra = None
    if extra_keep is not None:
        extra_got = swap(extra_send, "c")
        extra = extra_keep.astype(F32) + extra_got.astype(F32)

    def block(index, half):
        rows = slice(64 * half, 64 * half + 64)
        return pick(keep, index)[rows].astype(F32) + pick(got, index)[rows].astype(F32)

    ends = []
    for half, first, second in ((0, 1, 3), (1, 3, 1)):
        parts = [block(x ^ first, half), block(x ^ 2, half)]
        mine = [block(x, half), block(x ^ second, half)]
        if extra is not None:
            own = extra[64 * half : 64 * half + 64]
            parts.append(own)
            mine.append(own)
        step = ring(jnp.concatenate(parts, axis=1).astype(BF16), "x", first).astype(F32)
        total = jnp.concatenate(mine, axis=1) + step
        step = ring(total[:, WIDE:].astype(BF16), "x", second).astype(F32)
        own = total[:, :WIDE] + step[:, :WIDE]
        if extra is not None:
            own = jnp.concatenate([own, total[:, 2 * WIDE :] + step[:, WIDE:]], axis=1)
        ends.append(own)
    low = h == 0
    last = swap(jnp.where(low, ends[1], ends[0]).astype(BF16), "h").astype(F32)
    return jnp.where(low, ends[0], ends[1]) + last


def redistribute(residual, target, h, c):
    both = jnp.concatenate([residual, target], axis=0)
    both = jnp.swapaxes(both, 1, 2).reshape(4, 2, 2, 64, COLS)
    near = pick(both, h, 2)
    far = swap(pick(both, 1 - h, 2), "h")
    got = swap(jnp.stack([pick(near, 1 - c, 1), pick(far, 1 - c, 1)]), "c")
    near, far = pick(near, c, 1), pick(far, c, 1)
    first = c == 0
    near = [jnp.where(first, near, got[0]), jnp.where(first, got[0], near)]
    far = [jnp.where(first, far, got[1]), jnp.where(first, got[1], far)]
    low = h == 0
    return jnp.concatenate(
        [jnp.where(low, n, f) for n, f in zip(near, far)]
        + [jnp.where(low, f, n) for n, f in zip(near, far)],
        axis=-1,
    )


def over_ring(value):
    return value + ring(value, "x", 1) + ring(value, "x", 2) + ring(value, "x", 3)


def normal_grad(summed, target_now, token_mask):
    sums = over_ring(
        jnp.stack([jnp.sum(summed * summed, axis=1), jnp.sum(target_now * summed, axis=1)])
    )
    rms = jnp.sqrt(sums[0] / D + epsilon)
    along = sums[1] / D / rms
    rms, along = rms[:, None], along[:, None]
    return (token_mask * (target_now - summed / rms * along) / rms).astype(BF16)


def in_order(own, other, index, axis):
    first = index == 0
    return jnp.stack([jnp.where(first, own, other), jnp.where(first, other, own)], axis=axis)


def to_owners(chunks, b, h):
    parts = [[None, None], [None, None]]
    for m1, m2 in itertools.product(range(2), range(2)):
        pairs = [
            (flat(y, b_, a, x, h_, c), flat(x, b_ ^ m1, c, y, h_ ^ m2, a))
            for y, b_, a, x, h_, c in devices()
        ]
        parts[m1][m2] = lax.ppermute(pick(chunks, b ^ m1), AXES, pairs)
    held = jnp.stack(
        [in_order(p.reshape(2, 64, COLS), q.reshape(2, 64, COLS), h, 1).reshape(TOK, COLS) for p, q in parts]
    )
    near = [held] + [ring(held, "x", k) for k in (1, 2, 3)]
    return near + [swap(v, "c") for v in near]


def gather_rows(rows):
    return jnp.stack([rows] + [line(rows, k) for k in (1, 2, 3)])


def pack(block):
    top, rest = block[:, :128], block[:, 128:]
    last = rest[336:]
    groups = [
        jnp.concatenate([rest[112 * q : 112 * q + 112], last[:, 32 * q : 32 * q + 32]], axis=1)
        for q in range(3)
    ]
    return jnp.concatenate([top] + groups, axis=0)


def unpack(block):
    groups = [block[448 + 112 * q : 560 + 112 * q] for q in range(3)]
    last = jnp.concatenate([g[:, 96:] for g in groups], axis=1)
    rest = jnp.concatenate([g[:, :96] for g in groups] + [last], axis=0)
    return jnp.concatenate([block[:ROWS], rest], axis=1)


def outer_kernel(place, position, arrival, factors, slow_ref, held_ref, *refs):
    grads = refs[:16]
    rows = refs[16:24]
    out_ref, slow_out, held_out, g_ref, d_ref, s_ref, m_ref, sems = refs[24:]
    copies = [
        pltpu.make_async_copy(grads[8 * i + j], g_ref.at[j, :, i], sems.at[8 * i + j])
        for i in range(ITERS)
        for j in range(8)
    ]
    for copy in copies:
        copy.start()
    s_ref[...] = pack(slow_ref[...])
    m_ref[...] = pack(held_ref[...])
    for copy in copies:
        copy.wait()
    scale = inner_rate / math.sqrt(FF)
    y, b, a, x, c = (place[i] for i in range(5))
    for ky, slot in ((0, 0), (1, 1), (3, 2), (2, 3)):
        for kz in range(4):
            ry, rb, ra = y ^ ky, b ^ (kz // 2), a ^ (kz % 2)
            replica = ry * 4 + rb * 2 + ra
            buffer = (ra ^ c) * 4 + (ry ^ x)
            parts = []
            for half in range(2):
                block = rows[4 * half + slot]
                total = jnp.dot(
                    block[kz, :, :TOK], g_ref[buffer, rb ^ b, 0], preferred_element_type=F32
                ) + jnp.dot(
                    block[kz, :, TOK:], g_ref[buffer, rb ^ b, 1], preferred_element_type=F32
                )
                parts.append(total)
            d_ref[position[replica]] = pack(jnp.concatenate(parts, axis=0) * scale)

    def step(k, _):
        factor = factors[k]
        target = arrival[k]
        for at in range(0, PACKED, 112):
            here = pl.ds(at, 112)
            grad = d_ref[k, here] * factor
            held = momentum_decay * m_ref[here] + grad
            slow = s_ref[here] - outer_rate * (grad + momentum_decay * held)
            m_ref[here] = held
            s_ref[here] = slow
            out_ref[target, here] = slow.astype(BF16)
        return 0

    lax.fori_loop(0, REPLICAS, step, 0)
    slow_out[...] = unpack(s_ref[...])
    held_out[...] = unpack(m_ref[...])


def outer(place, position, arrival, factors, slow, held, grads, rows):
    smem = pl.BlockSpec(memory_space=pltpu.SMEM)
    vmem = pl.BlockSpec(memory_space=pltpu.VMEM)
    return pl.pallas_call(
        outer_kernel,
        in_specs=[smem] * 4 + [vmem] * 2 + [pl.BlockSpec(memory_space=pl.ANY)] * 16 + [vmem] * 8,
        out_specs=[vmem] * 3,
        out_shape=[
            jax.ShapeDtypeStruct((REPLICAS, PACKED, 128), BF16),
            jax.ShapeDtypeStruct((ROWS, COLS), F32),
            jax.ShapeDtypeStruct((ROWS, COLS), F32),
        ],
        scratch_shapes=[
            pltpu.VMEM((8, 2, ITERS, TOK, COLS), BF16),
            pltpu.VMEM((REPLICAS, PACKED, 128), F32),
            pltpu.VMEM((PACKED, 128), F32),
            pltpu.VMEM((PACKED, 128), F32),
            pltpu.SemaphoreType.DMA((16,)),
        ],
        compiler_params=pltpu.CompilerParams(vmem_limit_bytes=56 << 20),
        name="outer",
    )(place, position, arrival, factors, slow, held, *grads, *rows)


def assemble_kernel(in_ref, out_ref):
    blocks = [unpack(in_ref[i].astype(F32)) for i in range(4)]
    out_ref[...] = jnp.concatenate(blocks, axis=1).astype(BF16)


def assemble(blocks):
    return pl.pallas_call(
        assemble_kernel,
        grid=(4,),
        in_specs=[pl.BlockSpec((4, PACKED, 128), lambda i: (i, 0, 0))],
        out_specs=pl.BlockSpec((ROWS, WIDE), lambda i: (0, i)),
        out_shape=jax.ShapeDtypeStruct((ROWS, D), BF16),
        compiler_params=pltpu.CompilerParams(vmem_limit_bytes=32 << 20),
        name="assemble",
    )(blocks)


def local(
    replica_weights, slow_weights, momentum, hidden, residual, target, arrival, staleness, live
):
    y, b, a, x, h, c = (lax.axis_index(name) for name in AXES)
    weights, features = replica_weights[0], hidden[0]

    by_core = features.reshape(ITERS, 2, 128, ROWS)
    others, mine = pick(by_core, 1 - c, 1), pick(by_core, c, 1)
    send_first = forward(others[0], weights)
    keep_first = forward(mine[0], weights)
    first_output = reduce_tokens(keep_first, send_first, None, None, x, h)
    send_second = forward(others[1], weights)
    keep_second = forward(mine[1], weights)
    cross = [
        (
            lax.dot_general(
                rows[1], features[0], (((1,), (1,)), ((), ())), preferred_element_type=F32
            )
            * (inner_rate / FF)
        ).astype(BF16)
        for rows in (mine, others)
    ]
    second = reduce_tokens(keep_second, send_second, cross[0], cross[1], x, h)
    second_output, cross_rows = second[:, :WIDE], second[:, WIDE:].astype(BF16)

    turned = jnp.transpose(features, (2, 0, 1)).reshape(ROWS, ITERS * TOK)
    rows = []
    for half, (near, next_) in enumerate(((1, 3), (3, 1))):
        own = gather_rows(turned[COLS * half : COLS * half + COLS])
        one = ring(own, "y", near)
        two = ring(own, "y", next_)
        both = ring(one, "y", next_)
        rows += [own, one, two, both] if near == 1 else [own, two, one, both]

    streams = redistribute(residual[0], target[0], h, c).astype(F32)
    slots = jnp.arange(REPLICAS, dtype=jnp.int32)
    live_count = jnp.sum(jnp.where(slots == y * 4 + b * 2 + a, live, 0))
    token = c * 128 + h * 64 + jnp.arange(64, dtype=jnp.int32)
    token_mask = (token < live_count).astype(F32)[:, None]

    first_grad = normal_grad(streams[0] + first_output, streams[2], token_mask)
    by_h = in_order(first_grad, swap(first_grad, "h"), h, 0)
    all_first = in_order(by_h, swap(by_h, "c"), c, 0).reshape(TOK, WIDE)
    change = jnp.dot(cross_rows, all_first, preferred_element_type=F32)
    second_grad = normal_grad(streams[1] + (second_output - change), streams[3], token_mask)

    first_chunks = pick(
        pick(all_first.reshape(2, 2, 64, 2, 2, COLS), h, 1), c, 3
    )
    first_chunks = jnp.transpose(first_chunks, (2, 0, 1, 3)).reshape(2, 128, COLS)
    by_core = second_grad.reshape(64, 2, 2, COLS)
    second_chunks = in_order(pick(by_core, c, 2), swap(pick(by_core, 1 - c, 2), "c"), c, 0)
    second_chunks = jnp.transpose(second_chunks, (2, 0, 1, 3)).reshape(2, 128, COLS)
    grads = to_owners(first_chunks, b, h) + to_owners(second_chunks, b, h)

    position = jnp.sum(jnp.where(arrival[None, :] == slots[:, None], slots[None, :], 0), axis=1)
    factors = 1.0 / (1.0 + staleness.astype(F32))
    place = jnp.stack([y, b, a, x, c]).astype(jnp.int32)
    results, slow_after, momentum_after = outer(
        place, position.astype(jnp.int32), arrival, factors, slow_weights, momentum, grads, rows
    )
    back = lax.all_to_all(results, ("y", "b", "a"), 0, 0, tiled=True)
    return (assemble(back)[None], slow_after, momentum_after)


def solution(mesh):
    rep, tp = AXES[:3], AXES[3:]
    fine = Mesh(mesh.devices.reshape(SIZES), AXES)
    return jax.shard_map(
        local,
        mesh=fine,
        in_specs=(
            P(rep, tp, None),
            P(tp, rep),
            P(tp, rep),
            P(rep, None, None, tp),
            P(rep, None, tp, None),
            P(rep, None, tp, None),
            P(),
            P(),
            P(),
        ),
        out_specs=(P(rep, tp, None), P(tp, rep), P(tp, rep)),
        check_vma=False,
    )
```

```python
import itertools
import math

import jax
import jax.numpy as jnp
from jax import lax
from jax.experimental import pallas as pl
from jax.experimental.pallas import tpu as pltpu
from jax.sharding import Mesh
from jax.sharding import PartitionSpec as P

D = 3584
FF = 7168
TOK = 256
ITERS = 2
REPLICAS = 16
ROWS = 448
COLS = 224
WIDE = 896
PACKED = 784

inner_rate = 2.0
outer_rate = 0.7
momentum_decay = 0.9
epsilon = 1e-06

AXES = ("y", "b", "a", "x", "h", "c")
SIZES = (4, 2, 2, 4, 2, 2)
F32 = jnp.float32
BF16 = jnp.bfloat16


def flat(*where):
    index = 0
    for size, place in zip(SIZES, where):
        index = index * size + place
    return index


def devices():
    return itertools.product(*map(range, SIZES))


def swap(value, axis):
    return lax.ppermute(value, axis, [(0, 1), (1, 0)])


def ring(value, axis, mask):
    return lax.ppermute(value, axis, [(i, i ^ mask) for i in range(4)])


def line(value, mask):
    return lax.ppermute(value, ("b", "a"), [(i, i ^ mask) for i in range(4)])


def pick(array, index, axis=0):
    return lax.dynamic_index_in_dim(array, index, axis, keepdims=False)


def forward_kernel(rows_ref, weights_ref, out_ref):
    out_ref[0] = (
        jnp.dot(rows_ref[...], weights_ref[...], preferred_element_type=F32)
        * (1.0 / math.sqrt(FF))
    ).astype(BF16)


def forward(rows, weights):
    count = rows.shape[0]
    return pl.pallas_call(
        forward_kernel,
        grid=(4,),
        in_specs=[
            pl.BlockSpec((count, ROWS), lambda i: (0, 0)),
            pl.BlockSpec((ROWS, WIDE), lambda i: (0, i)),
        ],
        out_specs=pl.BlockSpec((1, count, WIDE), lambda i: (i, 0, 0)),
        out_shape=jax.ShapeDtypeStruct((4, count, WIDE), BF16),
        cost_estimate=pl.CostEstimate(
            flops=2 * count * ROWS * D, bytes_accessed=2 * ROWS * D, transcendentals=0
        ),
        compiler_params=pltpu.CompilerParams(vmem_limit_bytes=32 << 20),
        name="forward",
    )(rows, weights)


def after(value, *others):
    return lax.optimization_barrier((value, *others))[0]


def away_kernel(place, keep_ref, got_ref, extra_ref, first_ref, second_ref):
    x = place[0]
    for half, out, near in ((0, first_ref, 1), (1, second_ref, 3)):
        for j, mask in enumerate((near, 2)):
            for i in range(ITERS):
                rows = pl.ds(128 * i + 64 * half, 64)
                block = keep_ref[x ^ mask, rows].astype(F32) + got_ref[x ^ mask, rows].astype(F32)
                at = (j * ITERS + i) * WIDE
                out[:, at : at + WIDE] = block.astype(BF16)
        out[:, 2 * ITERS * WIDE :] = extra_ref[pl.ds(64 * half, 64)].astype(BF16)


def split_away(x, keep, got, extra):
    shape = jax.ShapeDtypeStruct((64, 2 * ITERS * WIDE + TOK), BF16)
    vmem = pl.BlockSpec(memory_space=pltpu.VMEM)
    return pl.pallas_call(
        away_kernel,
        in_specs=[pl.BlockSpec(memory_space=pltpu.SMEM)] + [vmem] * 3,
        out_specs=[vmem] * 2,
        out_shape=[shape, shape],
        compiler_params=pltpu.CompilerParams(vmem_limit_bytes=24 << 20),
        name="split_away",
    )(x.astype(jnp.int32).reshape(1), keep, got, extra)


def own_blocks(keep, got, extra, x, half, second):
    def block(step, index):
        rows = slice(128 * step + 64 * half, 128 * step + 64 * half + 64)
        return pick(keep, index)[rows].astype(F32) + pick(got, index)[rows].astype(F32)

    mine = [block(i, x) for i in range(ITERS)] + [block(i, x ^ second) for i in range(ITERS)]
    return jnp.concatenate(mine + [extra[64 * half : 64 * half + 64]], axis=1)


def turn(near, far, c):
    both = jnp.stack([near, far])
    both = jnp.swapaxes(both, 2, 3).reshape(2, 4, 2, 64, COLS)
    return pick(both, c, 2), pick(both, 1 - c, 2)


def features_in_order(own, got, h, c):
    first, low = c == 0, h == 0
    pairs = [jnp.where(first, own, got), jnp.where(first, got, own)]
    return jnp.concatenate(
        [jnp.where(low, p[0], p[1]) for p in pairs] + [jnp.where(low, p[1], p[0]) for p in pairs],
        axis=-1,
    )


def over_ring(value):
    return value + ring(value, "x", 1) + ring(value, "x", 2) + ring(value, "x", 3)


def sums_of(summed, target_now):
    return jnp.stack([jnp.sum(summed * summed, axis=1), jnp.sum(target_now * summed, axis=1)])


def normal_grad(summed, target_now, sums, token_mask):
    rms = jnp.sqrt(sums[0] / D + epsilon)
    along = sums[1] / D / rms
    rms, along = rms[:, None], along[:, None]
    return (token_mask * (target_now - summed / rms * along) / rms).astype(BF16)


def in_order(own, other, index, axis):
    first = index == 0
    return jnp.stack([jnp.where(first, own, other), jnp.where(first, other, own)], axis=axis)


def to_owners(chunks, b, h):
    parts = [[None, None], [None, None]]
    for m1, m2 in itertools.product(range(2), range(2)):
        pairs = [
            (flat(y, b_, a, x, h_, c), flat(x, b_ ^ m1, c, x ^ y, h_ ^ m2, a))
            for y, b_, a, x, h_, c in devices()
        ]
        part = lax.ppermute(pick(chunks, b ^ m1), AXES, pairs)
        parts[m1][m2] = part.reshape(ITERS, 2, 64, COLS)
    return [in_order(p, q, h, 1).reshape(ITERS, TOK, COLS) for p, q in parts]


def to_all(held):
    grads = []
    one = [ring(held[0], "x", 1), ring(held[1], "x", 3)]
    pairs = [jnp.stack([v, w]) for v, w in zip(held, one)]
    two = [ring(pairs[0], "x", 3), ring(pairs[1], "x", 1)]
    for i in range(2):
        grads += [pairs[i], two[i], swap(pairs[i], "c"), swap(two[i], "c")]
    return grads


def pack(block):
    top, rest = block[:, :128], block[:, 128:]
    last = rest[336:]
    groups = [
        jnp.concatenate([rest[112 * q : 112 * q + 112], last[:, 32 * q : 32 * q + 32]], axis=1)
        for q in range(3)
    ]
    return jnp.concatenate([top] + groups, axis=0)


def unpack(block):
    groups = [block[448 + 112 * q : 560 + 112 * q] for q in range(3)]
    last = jnp.concatenate([g[:, 96:] for g in groups], axis=1)
    rest = jnp.concatenate([g[:, :96] for g in groups] + [last], axis=0)
    return jnp.concatenate([block[:ROWS], rest], axis=1)


def outer_kernel(place, position, arrival, factors, slow_ref, held_ref, *refs):
    grads = refs[:8]
    rows = refs[8:16]
    out_ref, slow_out, held_out, g_ref, d_ref, s_ref, m_ref, sems = refs[16:]
    copies = []
    for part in range(2):
        for core in range(2):
            for far in range(2):
                source = grads[part * 4 + core * 2 + far]
                for i in range(2):
                    if part == 0:
                        mask = (0, 1)[i] ^ (3 * far)
                    else:
                        mask = (0, 3)[i] ^ far
                    copies.append(
                        pltpu.make_async_copy(
                            source.at[i], g_ref.at[core, mask, part], sems.at[len(copies)]
                        )
                    )
    for copy in copies:
        copy.start()
    s_ref[...] = pack(slow_ref[...])
    m_ref[...] = pack(held_ref[...])
    for copy in copies:
        copy.wait()
    scale = inner_rate / math.sqrt(FF)
    y, b, a, c = place[0], place[1], place[2], place[3]
    x = place[4]
    for ky in range(4):
        for kz in range(4):
            block = rows[(kz // 2) * 4 + ky].at[kz % 2]
            ry, rb, ra = y ^ ky, b ^ (kz // 2), a ^ (kz % 2)
            slot = ry ^ y ^ x
            total = jnp.dot(
                block[:, :TOK], g_ref[ra ^ c, slot, rb ^ b, 0], preferred_element_type=F32
            ) + jnp.dot(
                block[:, TOK:], g_ref[ra ^ c, slot, rb ^ b, 1], preferred_element_type=F32
            )
            d_ref[position[ry * 4 + rb * 2 + ra]] = pack(total * scale)

    def step(k, _):
        factor = factors[k]
        target = arrival[k]
        for at in range(0, PACKED, 112):
            here = pl.ds(at, 112)
            grad = d_ref[k, here] * factor
            held = momentum_decay * m_ref[here] + grad
            slow = s_ref[here] - outer_rate * (grad + momentum_decay * held)
            m_ref[here] = held
            s_ref[here] = slow
            out_ref[target, here] = slow.astype(BF16)
        return 0

    lax.fori_loop(0, REPLICAS, step, 0)
    slow_out[...] = unpack(s_ref[...])
    held_out[...] = unpack(m_ref[...])


def outer(place, position, arrival, factors, slow, held, grads, rows):
    smem = pl.BlockSpec(memory_space=pltpu.SMEM)
    vmem = pl.BlockSpec(memory_space=pltpu.VMEM)
    return pl.pallas_call(
        outer_kernel,
        in_specs=[smem] * 4 + [vmem] * 2 + [pl.BlockSpec(memory_space=pl.ANY)] * 8 + [vmem] * 8,
        out_specs=[vmem] * 3,
        out_shape=[
            jax.ShapeDtypeStruct((REPLICAS, PACKED, 128), BF16),
            jax.ShapeDtypeStruct((ROWS, COLS), F32),
            jax.ShapeDtypeStruct((ROWS, COLS), F32),
        ],
        scratch_shapes=[
            pltpu.VMEM((2, 4, 2, ITERS, TOK, COLS), BF16),
            pltpu.VMEM((REPLICAS, PACKED, 128), F32),
            pltpu.VMEM((PACKED, 128), F32),
            pltpu.VMEM((PACKED, 128), F32),
            pltpu.SemaphoreType.DMA((16,)),
        ],
        compiler_params=pltpu.CompilerParams(vmem_limit_bytes=56 << 20),
        name="outer",
    )(place, position, arrival, factors, slow, held, *grads, *rows)


def assemble_kernel(in_ref, out_ref):
    blocks = [unpack(in_ref[i].astype(F32)) for i in range(4)]
    out_ref[...] = jnp.concatenate(blocks, axis=1).astype(BF16)


def assemble(blocks):
    return pl.pallas_call(
        assemble_kernel,
        grid=(4,),
        in_specs=[pl.BlockSpec((4, PACKED, 128), lambda i: (i, 0, 0))],
        out_specs=pl.BlockSpec((ROWS, WIDE), lambda i: (0, i)),
        out_shape=jax.ShapeDtypeStruct((ROWS, D), BF16),
        compiler_params=pltpu.CompilerParams(vmem_limit_bytes=32 << 20),
        name="assemble",
    )(blocks)


def local(
    replica_weights, slow_weights, momentum, hidden, residual, target, arrival, staleness, live
):
    y, b, a, x, h, c = (lax.axis_index(name) for name in AXES)
    weights, features = replica_weights[0], hidden[0]

    by_core = features.reshape(ITERS, 2, 2, 64, ROWS)
    others = pick(by_core, 1 - c, 2).reshape(TOK, ROWS)
    mine = pick(by_core, c, 2).reshape(TOK, ROWS)
    send = forward(others, weights)
    got = swap(send, "c")
    keep = forward(after(mine, send), weights)

    by_h = [v.reshape(ITERS, COLS, 2, 128) for v in after((residual[0], target[0]), keep)]
    far = swap(jnp.concatenate([pick(v, 1 - h, 2) for v in by_h]), "h")

    turned = jnp.transpose(after(features, keep), (2, 0, 1)).reshape(ROWS, ITERS * TOK)
    one_z = line(turned, 1)

    cross = [
        (
            lax.dot_general(
                rows[128:], features[0], (((1,), (1,)), ((), ())), preferred_element_type=F32
            )
            * (inner_rate / FF)
        ).astype(BF16)
        for rows in (mine, others)
    ]
    extra = cross[0].astype(F32) + swap(cross[1], "c").astype(F32)
    away = split_away(x, keep, got, extra)
    steps = [ring(v, "x", k) for v, k in zip(away, (1, 3))]
    keep, got, extra = after((keep, got, extra), *away)
    owns = [
        own_blocks(keep, got, extra, x, half, second) for half, second in zip((0, 1), (3, 1))
    ]
    two_z = line(after(turned, *away), 2)

    steps, one_z, far = lax.optimization_barrier((steps, one_z, far))
    totals = [own + step.astype(F32) for own, step in zip(owns, steps)]
    cut = ITERS * WIDE
    away = [v[:, cut:].astype(BF16) for v in totals]
    steps = [ring(v, "x", k) for v, k in zip(away, (3, 1))]
    upper = jnp.stack([turned, after(one_z, *away)])
    upper_one, upper_two = ring(upper, "y", 1), ring(upper, "y", 3)
    near = jnp.concatenate([pick(v, h, 2) for v in after(by_h, *away)])
    near, give = turn(near, far, c)
    streams = features_in_order(near, swap(give, "c"), h, c).astype(F32)

    steps, two_z = lax.optimization_barrier((steps, two_z))
    totals = [
        jnp.concatenate([v[:, :cut], v[:, 2 * cut :]], axis=1) + step.astype(F32)
        for v, step in zip(totals, steps)
    ]
    low = h == 0
    away = jnp.where(low, totals[1], totals[0]).astype(BF16)
    last = swap(away, "h")
    three_z = line(after(turned, away), 3)
    last, upper_one, upper_two = lax.optimization_barrier((last, upper_one, upper_two))
    output = jnp.where(low, totals[0], totals[1]) + last.astype(F32)
    first_output, second_output = output[:, :WIDE], output[:, WIDE : 2 * WIDE]
    cross_rows = output[:, 2 * WIDE :].astype(BF16)

    slots = jnp.arange(REPLICAS, dtype=jnp.int32)
    live_count = jnp.sum(jnp.where(slots == y * 4 + b * 2 + a, live, 0))
    token = h * 128 + c * 64 + jnp.arange(64, dtype=jnp.int32)
    token_mask = (token < live_count).astype(F32)[:, None]

    summed = streams[0] + first_output
    sums = sums_of(summed, streams[2])
    total = over_ring(sums)
    upper_both = ring(after(upper_one, sums), "y", 3)
    total, three_z = lax.optimization_barrier((total, three_z))
    first_grad = normal_grad(summed, streams[2], total, token_mask)
    by_h = in_order(first_grad, swap(first_grad, "h"), h, 0)
    lower = jnp.stack(after([two_z, three_z], first_grad))
    lower_one, lower_two = ring(lower, "y", 3), ring(lower, "y", 1)
    all_first = in_order(by_h, swap(by_h, "c"), c, 1)
    change = jnp.dot(cross_rows, all_first.reshape(TOK, WIDE), preferred_element_type=F32)
    summed = streams[1] + (second_output - change)
    sums = sums_of(summed, streams[3])
    total = over_ring(sums)
    second_grad = normal_grad(summed, streams[3], total, token_mask)

    first_chunks = pick(after(all_first, sums), h, 0).reshape(2, 64, 2, 2, COLS)
    first_chunks = pick(first_chunks, c, 3)
    by_core = second_grad.reshape(64, 2, 2, COLS)
    second_chunks = in_order(pick(by_core, c, 2), swap(pick(by_core, 1 - c, 2), "c"), c, 0)
    chunks = jnp.stack([first_chunks, second_chunks]).reshape(ITERS, 128, 2, COLS)
    chunks = jnp.transpose(chunks, (2, 0, 1, 3))
    held = to_owners(chunks, b, h)
    held, lower_one, lower_two = lax.optimization_barrier((held, lower_one, lower_two))
    lower_both = ring(lower_one, "y", 1)
    grads = to_all(held)
    rows = [upper, upper_one, upper_both, upper_two, lower, lower_two, lower_both, lower_one]

    position = jnp.sum(jnp.where(arrival[None, :] == slots[:, None], slots[None, :], 0), axis=1)
    factors = 1.0 / (1.0 + staleness.astype(F32))
    place = jnp.stack([y, b, a, c, x]).astype(jnp.int32)
    results, slow_after, momentum_after = outer(
        place, position.astype(jnp.int32), arrival, factors, slow_weights, momentum, grads, rows
    )
    back = lax.all_to_all(results, ("y", "b", "a"), 0, 0, tiled=True)
    return (assemble(back)[None], slow_after, momentum_after)


def solution(mesh):
    rep, tp = AXES[:3], AXES[3:]
    fine = Mesh(mesh.devices.reshape(SIZES), AXES)
    return jax.shard_map(
        local,
        mesh=fine,
        in_specs=(
            P(rep, tp, None),
            P(tp, rep),
            P(tp, rep),
            P(rep, None, None, tp),
            P(rep, None, tp, None),
            P(rep, None, tp, None),
            P(),
            P(),
            P(),
        ),
        out_specs=(P(rep, tp, None), P(tp, rep), P(tp, rep)),
        check_vma=False,
    )
```

```python
import itertools
import math

import jax
import jax.numpy as jnp
from jax import lax
from jax.experimental import pallas as pl
from jax.experimental.pallas import tpu as pltpu
from jax.sharding import Mesh
from jax.sharding import PartitionSpec as P

D = 3584
FF = 7168
TOK = 256
ITERS = 2
REPLICAS = 16
ROWS = 448
COLS = 224
WIDE = 896
PACKED = 784

inner_rate = 2.0
outer_rate = 0.7
momentum_decay = 0.9
epsilon = 1e-06

AXES = ("y", "b", "a", "x", "h", "c")
SIZES = (4, 2, 2, 4, 2, 2)
F32 = jnp.float32
BF16 = jnp.bfloat16


def flat(*where):
    index = 0
    for size, place in zip(SIZES, where):
        index = index * size + place
    return index


def devices():
    return itertools.product(*map(range, SIZES))


def swap(value, axis):
    return lax.ppermute(value, axis, [(0, 1), (1, 0)])


def ring(value, axis, mask):
    return lax.ppermute(value, axis, [(i, i ^ mask) for i in range(4)])


def line(value, mask):
    return lax.ppermute(value, ("b", "a"), [(i, i ^ mask) for i in range(4)])


def pick(array, index, axis=0):
    return lax.dynamic_index_in_dim(array, index, axis, keepdims=False)


def forward_kernel(which, rows_ref, features_ref, weights_ref, out_ref, cross_ref):
    rows = rows_ref[...].reshape(TOK, ROWS)
    out_ref[0] = (
        jnp.dot(rows, weights_ref[...], preferred_element_type=F32) * (1.0 / math.sqrt(FF))
    ).astype(BF16)

    @pl.when(pl.program_id(0) == 3)
    def _():
        cross = lax.dot_general(
            rows[128:],
            features_ref[...].reshape(TOK, ROWS),
            (((1,), (1,)), ((), ())),
            preferred_element_type=F32,
        )
        cross_ref[...] = (cross * (inner_rate / FF)).astype(BF16)


def forward(which, features, weights):
    by_core = features.reshape(ITERS, 2, 2, 64, ROWS)
    return pl.pallas_call(
        forward_kernel,
        grid_spec=pltpu.PrefetchScalarGridSpec(
            num_scalar_prefetch=1,
            grid=(4,),
            in_specs=[
                pl.BlockSpec((ITERS, 2, 1, 64, ROWS), lambda i, which: (0, 0, which[0], 0, 0)),
                pl.BlockSpec((1, 2, 2, 64, ROWS), lambda i, which: (0, 0, 0, 0, 0)),
                pl.BlockSpec((ROWS, WIDE), lambda i, which: (0, i)),
            ],
            out_specs=[
                pl.BlockSpec((1, TOK, WIDE), lambda i, which: (i, 0, 0)),
                pl.BlockSpec((128, TOK), lambda i, which: (0, 0)),
            ],
        ),
        out_shape=[
            jax.ShapeDtypeStruct((4, TOK, WIDE), BF16),
            jax.ShapeDtypeStruct((128, TOK), BF16),
        ],
        compiler_params=pltpu.CompilerParams(vmem_limit_bytes=32 << 20),
        name="forward",
    )(which.astype(jnp.int32).reshape(1), by_core, by_core, weights)


def transpose_kernel(features_ref, out_ref):
    for i in range(ITERS):
        block = features_ref[i].astype(F32)
        out_ref[:, TOK * i : TOK * i + TOK] = jnp.swapaxes(block, 0, 1).astype(BF16)


def transpose_features(features):
    return pl.pallas_call(
        transpose_kernel,
        out_shape=jax.ShapeDtypeStruct((ROWS, ITERS * TOK), BF16),
        compiler_params=pltpu.CompilerParams(vmem_limit_bytes=16 << 20),
        name="transpose_features",
    )(features)


def divide_kernel(place, residual_ref, target_ref, near_ref, far_ref):
    for out, index in ((near_ref, place[0]), (far_ref, 1 - place[0])):
        lanes = pl.ds(pl.multiple_of(128 * index, 128), 128)
        for i in range(ITERS):
            out[i] = residual_ref[i, :, lanes]
            out[ITERS + i] = target_ref[i, :, lanes]


def divide(h, residual, target):
    vmem = pl.BlockSpec(memory_space=pltpu.VMEM)
    return pl.pallas_call(
        divide_kernel,
        in_specs=[pl.BlockSpec(memory_space=pltpu.SMEM), vmem, vmem],
        out_shape=[jax.ShapeDtypeStruct((2 * ITERS, COLS, 128), BF16)] * 2,
        compiler_params=pltpu.CompilerParams(vmem_limit_bytes=16 << 20),
        name="divide",
    )(h.astype(jnp.int32).reshape(1), residual, target)


def turn_kernel(place, near_ref, far_ref, own_ref, give_ref, turned_ref):
    own = pl.ds(pl.multiple_of(64 * place[0], 64), 64)
    give = pl.ds(pl.multiple_of(64 * (1 - place[0]), 64), 64)
    for j, source in enumerate((near_ref, far_ref)):
        for i in range(2 * ITERS):
            turned_ref[...] = jnp.swapaxes(source[i].astype(F32), 0, 1)
            own_ref[j, i] = turned_ref[own].astype(BF16)
            give_ref[j, i] = turned_ref[give].astype(BF16)


def turn(c, near, far):
    vmem = pl.BlockSpec(memory_space=pltpu.VMEM)
    return pl.pallas_call(
        turn_kernel,
        in_specs=[pl.BlockSpec(memory_space=pltpu.SMEM), vmem, vmem],
        out_shape=[jax.ShapeDtypeStruct((2, 2 * ITERS, 64, COLS), BF16)] * 2,
        scratch_shapes=[pltpu.VMEM((128, COLS), F32)],
        compiler_params=pltpu.CompilerParams(vmem_limit_bytes=16 << 20),
        name="turn",
    )(c.astype(jnp.int32).reshape(1), near, far)


def after(value, *others):
    return lax.optimization_barrier((value, *others))[0]


def away_kernel(place, keep_ref, got_ref, extra_ref, first_ref, second_ref):
    x = place[0]
    for half, out, near in ((0, first_ref, 1), (1, second_ref, 3)):
        for j, mask in enumerate((near, 2)):
            for i in range(ITERS):
                rows = pl.ds(128 * i + 64 * half, 64)
                block = keep_ref[x ^ mask, rows].astype(F32) + got_ref[x ^ mask, rows].astype(F32)
                at = (j * ITERS + i) * WIDE
                out[:, at : at + WIDE] = block.astype(BF16)
        out[:, 2 * ITERS * WIDE :] = extra_ref[pl.ds(64 * half, 64)].astype(BF16)


def split_away(x, keep, got, extra):
    shape = jax.ShapeDtypeStruct((64, 2 * ITERS * WIDE + TOK), BF16)
    vmem = pl.BlockSpec(memory_space=pltpu.VMEM)
    return pl.pallas_call(
        away_kernel,
        in_specs=[pl.BlockSpec(memory_space=pltpu.SMEM)] + [vmem] * 3,
        out_specs=[vmem] * 2,
        out_shape=[shape, shape],
        compiler_params=pltpu.CompilerParams(vmem_limit_bytes=24 << 20),
        name="split_away",
    )(x.astype(jnp.int32).reshape(1), keep, got, extra)


def own_blocks(keep, got, extra, x, half, second):
    def block(step, index):
        rows = slice(128 * step + 64 * half, 128 * step + 64 * half + 64)
        return pick(keep, index)[rows].astype(F32) + pick(got, index)[rows].astype(F32)

    mine = [block(i, x) for i in range(ITERS)] + [block(i, x ^ second) for i in range(ITERS)]
    return jnp.concatenate(mine + [extra[64 * half : 64 * half + 64]], axis=1)


def features_in_order(own, got, h, c):
    first, low = c == 0, h == 0
    pairs = [jnp.where(first, own, got), jnp.where(first, got, own)]
    return jnp.concatenate(
        [jnp.where(low, p[0], p[1]) for p in pairs] + [jnp.where(low, p[1], p[0]) for p in pairs],
        axis=-1,
    )


def over_ring(value):
    return value + ring(value, "x", 1) + ring(value, "x", 2) + ring(value, "x", 3)


def sums_of(summed, target_now):
    return jnp.stack([jnp.sum(summed * summed, axis=1), jnp.sum(target_now * summed, axis=1)])


def normal_grad(summed, target_now, sums, token_mask):
    rms = jnp.sqrt(sums[0] / D + epsilon)
    along = sums[1] / D / rms
    rms, along = rms[:, None], along[:, None]
    return (token_mask * (target_now - summed / rms * along) / rms).astype(BF16)


def in_order(own, other, index, axis):
    first = index == 0
    return jnp.stack([jnp.where(first, own, other), jnp.where(first, other, own)], axis=axis)


def to_owners(chunks, b, h):
    parts = [[None, None], [None, None]]
    for m1, m2 in itertools.product(range(2), range(2)):
        pairs = [
            (flat(y, b_, a, x, h_, c), flat(x, b_ ^ m1, c, x ^ y, h_ ^ m2, a))
            for y, b_, a, x, h_, c in devices()
        ]
        part = lax.ppermute(pick(chunks, b ^ m1), AXES, pairs)
        parts[m1][m2] = part.reshape(ITERS, 2, 64, COLS)
    return [in_order(p, q, h, 1).reshape(ITERS, TOK, COLS) for p, q in parts]


def to_all(held):
    grads = []
    one = [ring(held[0], "x", 1), ring(held[1], "x", 3)]
    pairs = [jnp.stack([v, w]) for v, w in zip(held, one)]
    two = [ring(pairs[0], "x", 3), ring(pairs[1], "x", 1)]
    for i in range(2):
        grads += [pairs[i], two[i], swap(pairs[i], "c"), swap(two[i], "c")]
    return grads


def pack(block):
    top, rest = block[:, :128], block[:, 128:]
    last = rest[336:]
    groups = [
        jnp.concatenate([rest[112 * q : 112 * q + 112], last[:, 32 * q : 32 * q + 32]], axis=1)
        for q in range(3)
    ]
    return jnp.concatenate([top] + groups, axis=0)


def unpack(block):
    groups = [block[448 + 112 * q : 560 + 112 * q] for q in range(3)]
    last = jnp.concatenate([g[:, 96:] for g in groups], axis=1)
    rest = jnp.concatenate([g[:, :96] for g in groups] + [last], axis=0)
    return jnp.concatenate([block[:ROWS], rest], axis=1)


def outer_kernel(place, position, arrival, factors, slow_ref, held_ref, *refs):
    rows, refs = refs[:8], refs[8:]
    grads = refs[:8]
    out_ref, slow_out, held_out, h_ref, g_ref, d_ref, s_ref, m_ref, h_sems, g_sems = refs[8:]
    y, b, a, c, x = (place[i] for i in range(5))
    grad_copies = []
    for part, core, far, i in itertools.product(range(2), repeat=4):
        mask = (0, 1)[i] ^ (3 * far) if part == 0 else (0, 3)[i] ^ far
        source = grads[part * 4 + core * 2 + far].at[i]
        target = g_ref.at[core, mask, part]
        grad_copies.append(pltpu.make_async_copy(source, target, g_sems.at[len(grad_copies)]))
    for copy in grad_copies:
        copy.start()
    order = list(itertools.product(range(2), range(4), range(2)))
    row_copies = [
        pltpu.make_async_copy(rows[4 * kb + ky].at[ka], h_ref.at[i], h_sems.at[i])
        for i, (kb, ky, ka) in enumerate(order)
    ]
    for copy in row_copies:
        copy.start()
    s_ref[...] = pack(slow_ref[...])
    m_ref[...] = pack(held_ref[...])
    for copy in grad_copies:
        copy.wait()
    scale = inner_rate / math.sqrt(FF)
    for first in range(0, REPLICAS, 4):
        for i in range(first, first + 4):
            row_copies[i].wait()
        for i in range(first, first + 4):
            kb, ky, ka = order[i]
            ry, ra = y ^ ky, a ^ ka
            total = jnp.dot(
                h_ref[i],
                g_ref[ra ^ c, ky ^ x, kb].reshape(ITERS * TOK, COLS),
                preferred_element_type=F32,
            )
            d_ref[position[ry * 4 + (b ^ kb) * 2 + ra]] = pack(total)

    for at in range(0, PACKED, 112):
        here = pl.ds(at, 112)
        slow, held = s_ref[here], m_ref[here]
        for k in range(REPLICAS):
            grad = d_ref[k, here] * (factors[k] * scale)
            held = momentum_decay * held + grad
            slow = slow - outer_rate * (grad + momentum_decay * held)
            out_ref[arrival[k], here] = slow.astype(BF16)
        s_ref[here] = slow
        m_ref[here] = held
    slow_out[...] = unpack(s_ref[...])
    held_out[...] = unpack(m_ref[...])


def outer(place, position, arrival, factors, slow, held, rows, grads):
    smem = pl.BlockSpec(memory_space=pltpu.SMEM)
    vmem = pl.BlockSpec(memory_space=pltpu.VMEM)
    return pl.pallas_call(
        outer_kernel,
        in_specs=[smem] * 4 + [vmem] * 2 + [pl.BlockSpec(memory_space=pl.ANY)] * 16,
        out_specs=[vmem] * 3,
        out_shape=[
            jax.ShapeDtypeStruct((REPLICAS, PACKED, 128), BF16),
            jax.ShapeDtypeStruct((ROWS, COLS), F32),
            jax.ShapeDtypeStruct((ROWS, COLS), F32),
        ],
        scratch_shapes=[
            pltpu.VMEM((REPLICAS, ROWS, ITERS * TOK), BF16),
            pltpu.VMEM((2, 4, 2, ITERS, TOK, COLS), BF16),
            pltpu.VMEM((REPLICAS, PACKED, 128), F32),
            pltpu.VMEM((PACKED, 128), F32),
            pltpu.VMEM((PACKED, 128), F32),
            pltpu.SemaphoreType.DMA((REPLICAS,)),
            pltpu.SemaphoreType.DMA((16,)),
        ],
        compiler_params=pltpu.CompilerParams(vmem_limit_bytes=56 << 20),
        name="outer",
    )(place, position, arrival, factors, slow, held, *rows, *grads)


def assemble_kernel(in_ref, out_ref):
    blocks = [unpack(in_ref[i].astype(F32)) for i in range(4)]
    out_ref[...] = jnp.concatenate(blocks, axis=1).astype(BF16)


def assemble(blocks):
    return pl.pallas_call(
        assemble_kernel,
        grid=(4,),
        in_specs=[pl.BlockSpec((4, PACKED, 128), lambda i: (i, 0, 0))],
        out_specs=pl.BlockSpec((ROWS, WIDE), lambda i: (0, i)),
        out_shape=jax.ShapeDtypeStruct((ROWS, D), BF16),
        compiler_params=pltpu.CompilerParams(vmem_limit_bytes=32 << 20),
        name="assemble",
    )(blocks)


def local(
    replica_weights, slow_weights, momentum, hidden, residual, target, arrival, staleness, live
):
    y, b, a, x, h, c = (lax.axis_index(name) for name in AXES)
    weights, features = replica_weights[0], hidden[0]

    turned = transpose_features(features)
    one_z = line(turned, 1)

    send, cross_send = forward(after(1 - c, turned), features, weights)
    got, cross_got = swap(send, "c"), swap(cross_send, "c")
    keep, cross_keep = forward(after(c, send), features, weights)

    extra = cross_keep.astype(F32) + cross_got.astype(F32)
    away = split_away(x, keep, got, extra)
    steps = [ring(v, "x", k) for v, k in zip(away, (1, 3))]
    keep, got, extra = after((keep, got, extra), *away)

    owns = [
        own_blocks(keep, got, extra, x, half, second) for half, second in zip((0, 1), (3, 1))
    ]
    two_z = line(after(turned, *away), 2)

    near, far = divide(h, *after((residual[0], target[0]), owns[0]))
    far = swap(far, "h")
    steps, one_z = lax.optimization_barrier((steps, one_z))
    totals = [own + step.astype(F32) for own, step in zip(owns, steps)]
    cut = ITERS * WIDE
    away = [v[:, cut:].astype(BF16) for v in totals]
    steps = [ring(v, "x", k) for v, k in zip(away, (3, 1))]
    upper = jnp.stack([turned, after(one_z, *away)])
    upper_one, upper_three = ring(upper, "y", 1), ring(upper, "y", 3)

    steps, two_z = lax.optimization_barrier((steps, two_z))
    near, give = turn(c, near, after(far, *away))
    streams = features_in_order(near, swap(give, "c"), h, c).astype(F32)
    totals = [
        jnp.concatenate([v[:, :cut], v[:, 2 * cut :]], axis=1) + step.astype(F32)
        for v, step in zip(totals, steps)
    ]
    low = h == 0
    away = jnp.where(low, totals[1], totals[0]).astype(BF16)
    last = swap(away, "h")
    three_z = line(after(turned, away), 3)
    last, upper_one, upper_three = lax.optimization_barrier((last, upper_one, upper_three))
    output = jnp.where(low, totals[0], totals[1]) + last.astype(F32)
    first_output, second_output = output[:, :WIDE], output[:, WIDE : 2 * WIDE]
    cross_rows = output[:, 2 * WIDE :].astype(BF16)

    slots = jnp.arange(REPLICAS, dtype=jnp.int32)
    live_count = jnp.sum(jnp.where(slots == y * 4 + b * 2 + a, live, 0))
    token = h * 128 + c * 64 + jnp.arange(64, dtype=jnp.int32)
    token_mask = (token < live_count).astype(F32)[:, None]

    summed = streams[0] + first_output
    sums = sums_of(summed, streams[2])
    total = over_ring(sums)
    upper_two = ring(after(upper_one, sums), "y", 3)
    total, three_z = lax.optimization_barrier((total, three_z))
    first_grad = normal_grad(summed, streams[2], total, token_mask)
    lower = jnp.stack(after([two_z, three_z], first_grad))
    lower_three, lower_one = ring(lower, "y", 3), ring(lower, "y", 1)
    by_h = in_order(first_grad, swap(first_grad, "h"), h, 0)
    all_first = in_order(by_h, swap(by_h, "c"), c, 1)
    change = jnp.dot(cross_rows, all_first.reshape(TOK, WIDE), preferred_element_type=F32)
    summed = streams[1] + (second_output - change)
    sums = sums_of(summed, streams[3])
    total = over_ring(sums)
    second_grad = normal_grad(summed, streams[3], total, token_mask)

    first_chunks = pick(after(all_first, sums), h, 0).reshape(2, 64, 2, 2, COLS)
    first_chunks = pick(first_chunks, c, 3)
    by_core = second_grad.reshape(64, 2, 2, COLS)
    second_chunks = in_order(pick(by_core, c, 2), swap(pick(by_core, 1 - c, 2), "c"), c, 0)
    chunks = jnp.stack([first_chunks, second_chunks]).reshape(ITERS, 128, 2, COLS)
    chunks = jnp.transpose(chunks, (2, 0, 1, 3))
    held = to_owners(chunks, b, h)
    held, lower_one, lower_three = lax.optimization_barrier((held, lower_one, lower_three))
    lower_two = ring(lower_three, "y", 1)
    grads = to_all(held)

    slots = jnp.arange(REPLICAS, dtype=jnp.int32)
    position = jnp.sum(jnp.where(arrival[None, :] == slots[:, None], slots[None, :], 0), axis=1)
    factors = 1.0 / (1.0 + staleness.astype(F32))
    place = jnp.stack([y, b, a, c, x]).astype(jnp.int32)
    results, slow_after, momentum_after = outer(
        place,
        position.astype(jnp.int32),
        arrival,
        factors,
        slow_weights,
        momentum,
        [upper, upper_one, upper_two, upper_three, lower, lower_one, lower_two, lower_three],
        grads,
    )
    back = lax.all_to_all(results, ("y", "b", "a"), 0, 0, tiled=True)
    return (assemble(back)[None], slow_after, momentum_after)


def solution(mesh):
    rep, tp = AXES[:3], AXES[3:]
    fine = Mesh(mesh.devices.reshape(SIZES), AXES)
    return jax.shard_map(
        local,
        mesh=fine,
        in_specs=(
            P(rep, tp, None),
            P(tp, rep),
            P(tp, rep),
            P(rep, None, None, tp),
            P(rep, None, tp, None),
            P(rep, None, tp, None),
            P(),
            P(),
            P(),
        ),
        out_specs=(P(rep, tp, None), P(tp, rep), P(tp, rep)),
        check_vma=False,
    )
```
